768 devices in a mesh: loop: 96 (over y, z), group: 8 (over x, core).
Axes of the slice: x: 4, y: 8, z: 12, core: 2. Of those that a mesh axis runs over, the one named last changes fastest.
Arguments:
- images: float32 [49152, 1152], P(('loop', 'group'))
- captions: float32 [49152, 1152], P(('loop', 'group'))
- labels: int32 [49152], P(('loop', 'group')), may hold values from 0 to 49151, as said below
- log_scale: float32 [1], replicated, may hold values from 1 to 2
- logit_bias: float32 [1], replicated, may hold values from -4 to -1
Outputs:
- grad_images: float32 [49152, 1152], P(('loop', 'group'))
- grad_captions: float32 [49152, 1152], P(('loop', 'group'))
The draws below stay inside these ranges and needn't reach their ends.
Inputs may be any that keep to these rules, and one draw needn't show every extreme that they name: `labels`: the matching text row of an image row in block p lies in block p, p - 1, ..., or p - 2, counted modulo 96.
All inputs are finite; a program needn't handle non-finite values.
Results may differ from the reference program's by a relative error of at most 0.0001.
Values sent between devices are 32-bit elements; how exact they have to be, the bound alone decides.
No kernel may reach another device: no remote copies, remote signals or barrier semaphores. Data moves between devices by JAX's collectives and lax.ppermute only.
A program may use at most 64 MiB of HBM per device.

```python
import jax
import jax.numpy as jnp
from jax import lax

D = 1152
IMG_DEV = 64
WIN = 3
TOTAL = 49152
N_LOOP = 96
N_GROUP = 8


def scaled_rows(key, low, high):
    row_key, entry_key = jax.random.split(key)
    scales = jnp.exp(jax.random.uniform(row_key, (TOTAL, 1), jnp.float32, jnp.log(low), jnp.log(high)))
    entries = jax.random.normal(entry_key, (TOTAL, D), jnp.float32)
    return entries * scales


def draw_images(key, part):
    key = jax.random.fold_in(key, 11)
    return scaled_rows(key, 0.01, 0.1)


def draw_captions(key, part):
    key = jax.random.fold_in(key, 23)
    return scaled_rows(key, 0.01, 0.1)


def draw_labels(key, part):
    key = jax.random.fold_in(key, 37)
    back_key, place_key = jax.random.split(key)
    block_rows = IMG_DEV * N_GROUP
    cycle_count = TOTAL // block_rows
    indices = jnp.arange(TOTAL, dtype=jnp.int32)
    owner = indices // block_rows
    backward = jax.random.randint(back_key, (TOTAL,), 0, WIN, jnp.int32)
    within = jax.random.randint(place_key, (TOTAL,), 0, block_rows, jnp.int32)
    result = (owner - backward) % cycle_count * block_rows + within
    result = result.at[0].set(0)
    result = result.at[TOTAL - 1].set(TOTAL - 1)
    return result


def setup_inputs(seed: int = 0) -> dict:
    key_list = jax.random.split(jax.random.key(seed), 6)
    images = draw_images(jax.random.fold_in(key_list[5], 71), 0)
    captions = draw_captions(jax.random.fold_in(key_list[5], 71), 0)
    labels = draw_labels(jax.random.fold_in(key_list[5], 71), 0)
    log_scale = jnp.clip(jax.random.uniform(key_list[3], (1,), jnp.float32, 1.0, 2.0), 1.0, 2.0)
    logit_bias = jnp.clip(jax.random.uniform(key_list[4], (1,), jnp.float32, -4.0, -1.0), -4.0, -1.0)
    return dict(images=images, captions=captions, labels=labels, log_scale=log_scale, logit_bias=logit_bias)


EPS = 1e-06

def normalize(values):
    inverse = lax.rsqrt(lax.optimization_barrier(jnp.sum(values * values, axis=-1, keepdims=True)) + EPS)
    return (values * inverse, inverse)

def unnormalize(unit, inverse, grad_unit):
    along = lax.optimization_barrier(jnp.sum(unit * grad_unit, axis=-1, keepdims=True))
    return inverse * (grad_unit - unit * along)

def reference(images, captions, labels, log_scale, logit_bias):
    block_rows = IMG_DEV * N_GROUP
    image_unit, image_inverse = normalize(images)
    text_unit, text_inverse = normalize(captions)
    image_blocks = image_unit.reshape(N_LOOP, block_rows, D)
    text_blocks = text_unit.reshape(N_LOOP, block_rows, D)
    label_rows = labels.reshape(N_LOOP, block_rows)
    temper = jnp.exp(log_scale[0])
    offset_bias = logit_bias[0]
    cycle_ids = jnp.arange(N_LOOP, dtype=jnp.int32)
    inside = jnp.arange(block_rows, dtype=jnp.int32)
    grad_image = jnp.zeros((N_LOOP, block_rows, D), jnp.float32)
    grad_text = jnp.zeros((N_LOOP, block_rows, D), jnp.float32)
    for stride in range(WIN):
        seen = jnp.roll(text_blocks, stride, axis=0)
        source = (cycle_ids - stride) % N_LOOP
        columns = source[:, None] * block_rows + inside[None, :]
        positive = (label_rows[:, :, None] == columns[:, None, :]).astype(jnp.float32)
        logits = temper * jnp.einsum('pid,pjd->pij', image_blocks, seen, precision=lax.Precision.HIGHEST) + offset_bias
        weights = jax.nn.sigmoid(logits) - positive
        grad_image = grad_image + temper * jnp.einsum('pij,pjd->pid', weights, seen, precision=lax.Precision.HIGHEST)
        part_text = temper * jnp.einsum('pij,pid->pjd', weights, image_blocks, precision=lax.Precision.HIGHEST)
        grad_text = grad_text + jnp.roll(part_text, -stride, axis=0)
    grad_images = unnormalize(image_unit, image_inverse, grad_image.reshape(-1, D))
    grad_captions = unnormalize(text_unit, text_inverse, grad_text.reshape(-1, D))
    return (grad_images, grad_captions)
```

```python
import jax
import jax.numpy as jnp
from jax import lax
from jax.experimental import pallas as pl
from jax.experimental.pallas import tpu as pltpu
from jax.sharding import PartitionSpec as P

WIN = 3
ROWS = 64
PACK = 72
D = 1152
X = 4
EPS = 1e-06
VMEM_LIMIT = 12 * 1024 * 1024


def along_loop(shard, by):
    count = lax.axis_size("loop")
    return lax.ppermute(shard, "loop", [(i, (i + by) % count) for i in range(count)])


def along_x(shard, by):
    count = lax.axis_size("group")
    return lax.ppermute(shard, "group", [(i, (i + 2 * by) % count) for i in range(count)])


def across_cores(shard):
    count = lax.axis_size("group")
    return lax.ppermute(shard, "group", [(i, i ^ 1) for i in range(count)])


def split(values):
    high = values.astype(jnp.bfloat16)
    low = (values - high.astype(jnp.float32)).astype(jnp.bfloat16)
    return high, low


NT = (((1,), (1,)), ((), ()))
NN = (((1,), (0,)), ((), ()))
TN = (((0,), (0,)), ((), ()))


def dot3(a, b, dims):
    def one(left, right):
        return lax.dot_general(left, right, dims, preferred_element_type=jnp.float32)

    return one(a[0], b[0]) + (one(a[0], b[1]) + one(a[1], b[0]))


def unit_rows(values):
    return values * lax.rsqrt(jnp.sum(values * values, axis=-1, keepdims=True) + EPS)


def label_row(packs):
    width = X * ROWS
    lane = lax.broadcasted_iota(jnp.int32, (1, width), 1)
    rows = [pack[ROWS : ROWS + 1, :width] for pack in packs]
    result = rows[X - 1]
    for k in range(X - 2, -1, -1):
        result = jnp.where(lane < (k + 1) * ROWS, rows[k], result)
    return result


def weights(texts, images, labels, scalars, base):
    def value(at):
        return scalars[at : at + 1, 0:1]

    sums = dot3(texts, images, NT)
    logits = value(0) * sums + value(1)
    row = lax.broadcasted_iota(jnp.int32, (WIN * ROWS, 1), 0)
    offset = jnp.where(
        row < ROWS,
        value(base),
        jnp.where(row < 2 * ROWS, value(base + 1) - ROWS, value(base + 2) - 2 * ROWS),
    )
    index = row.astype(jnp.float32) + offset
    positive = (index == labels).astype(jnp.float32)
    return split(jax.nn.sigmoid(logits) - positive)


def pack_kernel(images, labels, out, row, sem):
    images_in = pltpu.make_async_copy(images, out.at[pl.ds(0, ROWS), :], sem.at[0])
    label_in = pltpu.make_async_copy(labels, row, sem.at[1])
    images_in.start()
    label_in.start()
    label_in.wait()
    wide = row[...].astype(jnp.float32)
    wide = jnp.concatenate([wide, wide], axis=1)
    wide = jnp.concatenate([wide] * (D // (2 * ROWS)), axis=1)
    out[ROWS:, :] = jnp.broadcast_to(wide, (PACK - ROWS, D))
    images_in.wait()


def early_kernel(log_scale, logit_bias, places, t0, t1, scalars, units, t_high, t_low):
    for k, text in enumerate((t0, t1)):
        for r in range(0, ROWS, 32):
            at = k * ROWS + r
            unit = unit_rows(text[r : r + 32, :])
            units[at : at + 32, :] = unit
            t_high[at : at + 32, :], t_low[at : at + 32, :] = split(unit)

    def wide(value):
        return jnp.broadcast_to(value, (1, scalars.shape[1]))

    scalars[0:1, :] = jnp.exp(wide(log_scale[...]))
    scalars[1:2, :] = wide(logit_bias[...])
    for k in range(2 * WIN):
        scalars[2 + k : 3 + k, :] = wide(places[0:1, k : k + 1])


def late_kernel(t2, early_units, early_high, early_low, units, t_high, t_low):
    early = 2 * ROWS
    units[:early, :] = early_units[...]
    t_high[:early, :] = early_high[...]
    t_low[:early, :] = early_low[...]
    for r in range(0, ROWS, 32):
        at = early + r
        unit = unit_rows(t2[r : r + 32, :])
        units[at : at + 32, :] = unit
        t_high[at : at + 32, :], t_low[at : at + 32, :] = split(unit)


def own_kernel(
    scalars, p0, p1, p2, p3, t_high, t_low, x_high, x_low, labels, w_high, w_low, grad_text
):
    packs = (p0, p1, p2, p3)
    for k, pack in enumerate(packs):
        for r in range(0, ROWS, 32):
            at = k * ROWS + r
            x_high[at : at + 32, :], x_low[at : at + 32, :] = split(
                unit_rows(pack[r : r + 32, :])
            )
    row = label_row(packs)
    labels[...] = jnp.broadcast_to(row, labels.shape)
    images = (x_high[...], x_low[...])
    weight = weights((t_high[...], t_low[...]), images, row, scalars, 2)
    w_high[...], w_low[...] = weight
    grad_text[...] = dot3(weight, images, NN)


def cross_kernel(
    scalars, units, x_high, x_low, labels, t_high, t_low, w_high, w_low, grad_text
):
    for at in range(0, WIN * ROWS, 32):
        t_high[at : at + 32, :], t_low[at : at + 32, :] = split(units[at : at + 32, :])
    images = (x_high[...], x_low[...])
    weight = weights((t_high[...], t_low[...]), images, labels[0:1, :], scalars, 5)
    w_high[...], w_low[...] = weight
    grad_text[...] = dot3(weight, images, NN)


def image_kernel(
    w_high, w_low, t_high, t_low, ow_high, ow_low, ot_high, ot_low, o0, o1, o2, o3
):
    total = dot3((w_high[...], w_low[...]), (t_high[...], t_low[...]), TN) + dot3(
        (ow_high[...], ow_low[...]), (ot_high[...], ot_low[...]), TN
    )
    for k, out in enumerate((o0, o1, o2, o3)):
        out[...] = total[k * ROWS : (k + 1) * ROWS, :]


def last_kernel(own, other, after, out):
    at = (WIN - 1) * ROWS
    out[...] = own[at:, :] + other[at:, :]


def middle_kernel(own, other, back, out):
    out[...] = (own[ROWS : 2 * ROWS, :] + other[ROWS : 2 * ROWS, :]) + back[...]


def finish(values, grad, temper):
    inverse = lax.rsqrt(jnp.sum(values * values, axis=-1, keepdims=True) + EPS)
    unit = values * inverse
    grad = temper * grad
    along = jnp.sum(unit * grad, axis=-1, keepdims=True)
    return inverse * (grad - unit * along)


def final_kernel(
    scalars, images, captions, i0, i1, i2, i3, own, other, back, out_images, out_captions
):
    temper = scalars[0:1, 0:1]
    for r in range(0, ROWS, 32):
        at = slice(r, r + 32)
        grad = (own[at, :] + other[at, :]) + back[at, :]
        out_captions[at, :] = finish(captions[at, :], grad, temper)
        grad = (i0[at, :] + i1[at, :]) + (i2[at, :] + i3[at, :])
        out_images[at, :] = finish(images[at, :], grad, temper)


VMEM = pl.BlockSpec(memory_space=pltpu.VMEM)
HBM = pl.BlockSpec(memory_space=pl.ANY)


def f32(*shape):
    return jax.ShapeDtypeStruct(shape, jnp.float32)


def b16(*shape):
    return jax.ShapeDtypeStruct(shape, jnp.bfloat16)


def call(kernel, inputs, outs, products):
    return pl.pallas_call(
        kernel,
        in_specs=[VMEM] * inputs,
        out_specs=[VMEM] * len(outs),
        out_shape=outs,
        compiler_params=pltpu.CompilerParams(vmem_limit_bytes=VMEM_LIMIT),
        cost_estimate=pl.CostEstimate(
            flops=products * 3 * 2 * X * ROWS * WIN * ROWS * D,
            bytes_accessed=6 * X * ROWS * D * 4,
            transcendentals=X * ROWS * WIN * ROWS,
        ),
        name=kernel.__name__,
    )


def per_device(images, captions, labels, log_scale, logit_bias):
    position = lax.axis_index("loop")
    cycle_size = lax.axis_size("loop")
    member = lax.axis_index("group")
    members = lax.axis_size("group")
    images_all = X * ROWS
    texts_all = WIN * ROWS
    image_halves = [b16(images_all, D)] * 2
    text_halves = [b16(texts_all, D)] * 2

    text1 = along_loop(captions, 1)
    text2 = along_loop(text1, 1)
    pack = pl.pallas_call(
        pack_kernel,
        in_specs=[HBM, HBM],
        out_specs=VMEM,
        out_shape=f32(PACK, D),
        scratch_shapes=[pltpu.VMEM((1, ROWS), jnp.int32), pltpu.SemaphoreType.DMA((2,))],
        compiler_params=pltpu.CompilerParams(vmem_limit_bytes=VMEM_LIMIT),
        name="pack_kernel",
    )(images, labels[None, :])
    pack2, pack1, pack3 = (along_x(pack, k) for k in (2, 1, 3))

    places = []
    for who in (member, member ^ 1):
        for stride in range(WIN):
            source = (position - stride) % cycle_size
            places.append(source * (members * ROWS) + who * ROWS)
    places = jnp.stack(places).astype(jnp.float32)[None, :]
    scalars, *early = call(
        early_kernel, 5, [f32(8, 128), f32(2 * ROWS, D)] + [b16(2 * ROWS, D)] * 2, 60
    )(log_scale[None, :], logit_bias[None, :], places, captions, text1)
    units, t_high, t_low = call(late_kernel, 4, [f32(texts_all, D)] + text_halves, 0)(
        text2, *early
    )
    other_units = across_cores(units)

    weight_halves = [b16(texts_all, images_all)] * 2
    x_high, x_low, label_rows, w_high, w_low, own_text = call(
        own_kernel,
        7,
        image_halves + [f32(8, images_all)] + weight_halves + [f32(texts_all, D)],
        60,
    )(scalars, pack, pack1, pack2, pack3, t_high, t_low)
    ot_high, ot_low, ow_high, ow_low, other_text = call(
        cross_kernel, 5, text_halves + weight_halves + [f32(texts_all, D)], 2
    )(scalars, other_units, x_high, x_low, label_rows)
    other_text = across_cores(other_text)
    i0, i1, i2, i3 = call(image_kernel, 8, [f32(ROWS, D)] * X, 2)(
        w_high, w_low, t_high, t_low, ow_high, ow_low, ot_high, ot_low
    )
    back = pl.pallas_call(
        last_kernel,
        in_specs=[VMEM, VMEM, HBM],
        out_specs=VMEM,
        out_shape=f32(ROWS, D),
        compiler_params=pltpu.CompilerParams(vmem_limit_bytes=VMEM_LIMIT),
        name="last_kernel",
    )(own_text, other_text, i0)
    back = along_loop(back, -1)
    (back,) = call(middle_kernel, 3, [f32(ROWS, D)], 0)(own_text, other_text, back)
    back = along_loop(back, -1)
    i2, i1, i3 = along_x(i2, -2), along_x(i1, -1), along_x(i3, -3)

    first = pl.BlockSpec((ROWS, D), lambda i: (0, 0))
    return tuple(
        pl.pallas_call(
            final_kernel,
            grid=(1,),
            in_specs=[pl.BlockSpec((8, 128), lambda i: (0, 0))] + [first] * 9,
            out_specs=[first] * 2,
            out_shape=[f32(ROWS, D)] * 2,
            compiler_params=pltpu.CompilerParams(vmem_limit_bytes=VMEM_LIMIT),
            name="finish",
        )(scalars, images, captions, i0, i2, i1, i3, own_text, other_text, back)
    )


def solution(mesh):
    rows = P(("loop", "group"), None)
    placed = (rows, rows, P(("loop", "group")), P(), P())
    return jax.shard_map(
        per_device, mesh=mesh, in_specs=placed, out_specs=(rows, rows), check_vma=False
    )
```

```python
import jax
import jax.numpy as jnp
from jax import lax
from jax.experimental import pallas as pl
from jax.experimental.pallas import tpu as pltpu
from jax.sharding import PartitionSpec as P

WIN = 3
ROWS = 64
PACK = 72
D = 1152
X = 4
EPS = 1e-06
VMEM_LIMIT = 12 * 1024 * 1024


def along_loop(shard, by):
    count = lax.axis_size("loop")
    return lax.ppermute(shard, "loop", [(i, (i + by) % count) for i in range(count)])


def along_x(shard, by):
    count = lax.axis_size("group")
    pairs = [(i, (i + (2 * by if i % 2 == 0 else -2 * by)) % count) for i in range(count)]
    return lax.ppermute(shard, "group", pairs)


def across_cores(shard):
    count = lax.axis_size("group")
    return lax.ppermute(shard, "group", [(i, i ^ 1) for i in range(count)])


def split(values):
    high = values.astype(jnp.bfloat16)
    low = (values - high.astype(jnp.float32)).astype(jnp.bfloat16)
    return high, low


NT = (((1,), (1,)), ((), ()))
NN = (((1,), (0,)), ((), ()))
TN = (((0,), (0,)), ((), ()))


def dot3(a, b, dims):
    def one(left, right):
        return lax.dot_general(left, right, dims, preferred_element_type=jnp.float32)

    return one(a[0], b[0]) + (one(a[0], b[1]) + one(a[1], b[0]))


def unit_rows(values):
    return values * lax.rsqrt(jnp.sum(values * values, axis=-1, keepdims=True) + EPS)


def label_row(packs):
    width = X * ROWS
    lane = lax.broadcasted_iota(jnp.int32, (1, width), 1)
    rows = [pack[ROWS : ROWS + 1, :width] for pack in packs]
    result = rows[X - 1]
    for k in range(X - 2, -1, -1):
        result = jnp.where(lane < (k + 1) * ROWS, rows[k], result)
    return result


def weights(texts, images, labels, scalars, base):
    def value(at):
        return scalars[at : at + 1, 0:1]

    sums = dot3(texts, images, NT)
    logits = value(0) * sums + value(1)
    row = lax.broadcasted_iota(jnp.int32, (WIN * ROWS, 1), 0)
    offset = jnp.where(
        row < ROWS,
        value(base),
        jnp.where(row < 2 * ROWS, value(base + 1) - ROWS, value(base + 2) - 2 * ROWS),
    )
    index = row.astype(jnp.float32) + offset
    positive = (index == labels).astype(jnp.float32)
    return split(jax.nn.sigmoid(logits) - positive)


def pack_kernel(images, labels, out, row, sem):
    images_in = pltpu.make_async_copy(images, out.at[pl.ds(0, ROWS), :], sem.at[0])
    label_in = pltpu.make_async_copy(labels, row, sem.at[1])
    images_in.start()
    label_in.start()
    label_in.wait()
    wide = row[...].astype(jnp.float32)
    wide = jnp.concatenate([wide, wide], axis=1)
    wide = jnp.concatenate([wide] * (D // (2 * ROWS)), axis=1)
    out[ROWS:, :] = jnp.broadcast_to(wide, (PACK - ROWS, D))
    images_in.wait()


def early_kernel(log_scale, logit_bias, places, t0, t1, scalars, units, t_high, t_low):
    for k, text in enumerate((t0, t1)):
        for r in range(0, ROWS, 32):
            at = k * ROWS + r
            unit = unit_rows(text[r : r + 32, :])
            units[at : at + 32, :] = unit
            t_high[at : at + 32, :], t_low[at : at + 32, :] = split(unit)

    def wide(value):
        return jnp.full((1, scalars.shape[1]), value, jnp.float32)

    scalars[0:1, :] = jnp.exp(wide(log_scale[0]))
    scalars[1:2, :] = wide(logit_bias[0])
    for k in range(2 * WIN):
        scalars[2 + k : 3 + k, :] = wide(places[k].astype(jnp.float32))


def late_kernel(t2, early_units, early_high, early_low, units, t_high, t_low):
    early = 2 * ROWS
    units[:early, :] = early_units[...]
    t_high[:early, :] = early_high[...]
    t_low[:early, :] = early_low[...]
    for r in range(0, ROWS, 32):
        at = early + r
        unit = unit_rows(t2[r : r + 32, :])
        units[at : at + 32, :] = unit
        t_high[at : at + 32, :], t_low[at : at + 32, :] = split(unit)


def own_kernel(
    scalars, p0, p1, p2, p3, t_high, t_low, x_high, x_low, labels, w_high, w_low, grad_text
):
    packs = (p0, p1, p2, p3)
    for k, pack in enumerate(packs):
        for r in range(0, ROWS, 32):
            at = k * ROWS + r
            x_high[at : at + 32, :], x_low[at : at + 32, :] = split(
                unit_rows(pack[r : r + 32, :])
            )
    row = label_row(packs)
    labels[...] = jnp.broadcast_to(row, labels.shape)
    images = (x_high[...], x_low[...])
    weight = weights((t_high[...], t_low[...]), images, row, scalars, 2)
    w_high[...], w_low[...] = weight
    grad_text[...] = dot3(weight, images, NN)


def cross_kernel(
    scalars, units, x_high, x_low, labels, t_high, t_low, w_high, w_low, grad_text
):
    for at in range(0, WIN * ROWS, 32):
        t_high[at : at + 32, :], t_low[at : at + 32, :] = split(units[at : at + 32, :])
    images = (x_high[...], x_low[...])
    weight = weights((t_high[...], t_low[...]), images, labels[0:1, :], scalars, 5)
    w_high[...], w_low[...] = weight
    grad_text[...] = dot3(weight, images, NN)


def image_kernel(
    w_high, w_low, t_high, t_low, ow_high, ow_low, ot_high, ot_low, o0, o1, o2, o3
):
    total = dot3((w_high[...], w_low[...]), (t_high[...], t_low[...]), TN) + dot3(
        (ow_high[...], ow_low[...]), (ot_high[...], ot_low[...]), TN
    )
    for k, out in enumerate((o0, o1, o2, o3)):
        out[...] = total[k * ROWS : (k + 1) * ROWS, :]


def last_kernel(own, other, after, out):
    at = (WIN - 1) * ROWS
    out[...] = own[at:, :] + other[at:, :]


def middle_kernel(own, other, back, out):
    out[...] = (own[ROWS : 2 * ROWS, :] + other[ROWS : 2 * ROWS, :]) + back[...]


def add_kernel(a, b, out):
    out[...] = a[...] + b[...]


def finish(values, grad, temper):
    inverse = lax.rsqrt(jnp.sum(values * values, axis=-1, keepdims=True) + EPS)
    unit = values * inverse
    grad = temper * grad
    along = jnp.sum(unit * grad, axis=-1, keepdims=True)
    return inverse * (grad - unit * along)


def final_kernel(
    scalars, images, captions, i0, i1, i3, own, other, back, out_images, out_captions
):
    temper = scalars[0:1, 0:1]
    for r in range(0, ROWS, 32):
        at = slice(r, r + 32)
        grad = (own[at, :] + other[at, :]) + back[at, :]
        out_captions[at, :] = finish(captions[at, :], grad, temper)
        grad = (i0[at, :] + i1[at, :]) + i3[at, :]
        out_images[at, :] = finish(images[at, :], grad, temper)


SMEM = pl.BlockSpec(memory_space=pltpu.SMEM)
VMEM = pl.BlockSpec(memory_space=pltpu.VMEM)
HBM = pl.BlockSpec(memory_space=pl.ANY)


def f32(*shape):
    return jax.ShapeDtypeStruct(shape, jnp.float32)


def b16(*shape):
    return jax.ShapeDtypeStruct(shape, jnp.bfloat16)


def call(kernel, inputs, outs, products, smem=0):
    return pl.pallas_call(
        kernel,
        in_specs=[SMEM] * smem + [VMEM] * (inputs - smem),
        out_specs=[VMEM] * len(outs),
        out_shape=outs,
        compiler_params=pltpu.CompilerParams(vmem_limit_bytes=VMEM_LIMIT),
        cost_estimate=pl.CostEstimate(
            flops=products * 3 * 2 * X * ROWS * WIN * ROWS * D,
            bytes_accessed=6 * X * ROWS * D * 4,
            transcendentals=X * ROWS * WIN * ROWS,
        ),
        name=kernel.__name__,
    )


def per_device(images, captions, labels, log_scale, logit_bias):
    position = lax.axis_index("loop")
    cycle_size = lax.axis_size("loop")
    member = lax.axis_index("group")
    members = lax.axis_size("group")
    images_all = X * ROWS
    texts_all = WIN * ROWS
    image_halves = [b16(images_all, D)] * 2
    text_halves = [b16(texts_all, D)] * 2

    text1 = along_loop(captions, 1)
    text2 = along_loop(text1, 1)
    pack = pl.pallas_call(
        pack_kernel,
        in_specs=[HBM, HBM],
        out_specs=VMEM,
        out_shape=f32(PACK, D),
        scratch_shapes=[pltpu.VMEM((1, ROWS), jnp.int32), pltpu.SemaphoreType.DMA((2,))],
        compiler_params=pltpu.CompilerParams(vmem_limit_bytes=VMEM_LIMIT),
        name="pack_kernel",
    )(images, labels[None, :])
    pack1 = along_x(pack, 1)
    pack3 = along_x(pack, -1)
    pack2 = along_x(pack1, 1)

    places = []
    for who in (member, member ^ 1):
        for stride in range(WIN):
            source = (position - stride) % cycle_size
            places.append(source * (members * ROWS) + who * ROWS)
    places = jnp.stack(places)
    scalars, *early = call(
        early_kernel, 5, [f32(8, 128), f32(2 * ROWS, D)] + [b16(2 * ROWS, D)] * 2, 60, 3
    )(log_scale, logit_bias, places, captions, text1)
    units, t_high, t_low = call(late_kernel, 4, [f32(texts_all, D)] + text_halves, 0)(
        text2, *early
    )
    other_units = across_cores(units)

    weight_halves = [b16(texts_all, images_all)] * 2
    x_high, x_low, label_rows, w_high, w_low, own_text = call(
        own_kernel,
        7,
        image_halves + [f32(8, images_all)] + weight_halves + [f32(texts_all, D)],
        60,
    )(scalars, pack, pack1, pack2, pack3, t_high, t_low)
    ot_high, ot_low, ow_high, ow_low, other_text = call(
        cross_kernel, 5, text_halves + weight_halves + [f32(texts_all, D)], 2
    )(scalars, other_units, x_high, x_low, label_rows)
    other_text = across_cores(other_text)
    i0, i1, i2, i3 = call(image_kernel, 8, [f32(ROWS, D)] * X, 2)(
        w_high, w_low, t_high, t_low, ow_high, ow_low, ot_high, ot_low
    )
    back = pl.pallas_call(
        last_kernel,
        in_specs=[VMEM, VMEM, HBM],
        out_specs=VMEM,
        out_shape=f32(ROWS, D),
        compiler_params=pltpu.CompilerParams(vmem_limit_bytes=VMEM_LIMIT),
        name="last_kernel",
    )(own_text, other_text, i0)
    back = along_loop(back, -1)
    (back,) = call(middle_kernel, 3, [f32(ROWS, D)], 0)(own_text, other_text, back)
    back = along_loop(back, -1)
    (i1,) = call(add_kernel, 2, [f32(ROWS, D)], 0)(i1, along_x(i2, -1))
    i1 = along_x(i1, -1)
    i3 = along_x(i3, 1)

    first = pl.BlockSpec((ROWS, D), lambda i: (0, 0))
    return tuple(
        pl.pallas_call(
            final_kernel,
            grid=(1,),
            in_specs=[pl.BlockSpec((8, 128), lambda i: (0, 0))] + [first] * 8,
            out_specs=[first] * 2,
            out_shape=[f32(ROWS, D)] * 2,
            compiler_params=pltpu.CompilerParams(vmem_limit_bytes=VMEM_LIMIT),
            name="finish",
        )(scalars, images, captions, i0, i1, i3, own_text, other_text, back)
    )


def solution(mesh):
    rows = P(("loop", "group"), None)
    placed = (rows, rows, P(("loop", "group")), P(), P())
    return jax.shard_map(
        per_device, mesh=mesh, in_specs=placed, out_specs=(rows, rows), check_vma=False
    )
```

```python
import jax
import jax.numpy as jnp
from jax import lax
from jax.experimental import pallas as pl
from jax.experimental.pallas import tpu as pltpu
from jax.sharding import PartitionSpec as P

WIN = 3
ROWS = 64
PACK = 72
D = 1152
X = 4
EPS = 1e-06
VMEM_LIMIT = 12 * 1024 * 1024


def along_loop(shard, by):
    count = lax.axis_size("loop")
    return lax.ppermute(shard, "loop", [(i, (i + by) % count) for i in range(count)])


def along_x(shard, by):
    count = lax.axis_size("group")
    pairs = [(i, (i + (2 * by if i % 2 == 0 else -2 * by)) % count) for i in range(count)]
    return lax.ppermute(shard, "group", pairs)


def across_cores(shard):
    count = lax.axis_size("group")
    return lax.ppermute(shard, "group", [(i, i ^ 1) for i in range(count)])


def split(values):
    high = values.astype(jnp.bfloat16)
    low = (values - high.astype(jnp.float32)).astype(jnp.bfloat16)
    return high, low


NT = (((1,), (1,)), ((), ()))
NN = (((1,), (0,)), ((), ()))
TN = (((0,), (0,)), ((), ()))


def dot3(a, b, dims):
    def one(left, right):
        return lax.dot_general(left, right, dims, preferred_element_type=jnp.float32)

    return one(a[0], b[0]) + (one(a[0], b[1]) + one(a[1], b[0]))


def unit_rows(values):
    return values * lax.rsqrt(jnp.sum(values * values, axis=-1, keepdims=True) + EPS)


def label_row(packs):
    width = X * ROWS
    lane = lax.broadcasted_iota(jnp.int32, (1, width), 1)
    rows = [pack[ROWS : ROWS + 1, :width] for pack in packs]
    result = rows[X - 1]
    for k in range(X - 2, -1, -1):
        result = jnp.where(lane < (k + 1) * ROWS, rows[k], result)
    return result


def weights(texts, images, labels, scalars, base):
    def value(at):
        return scalars[at : at + 1, 0:1]

    sums = dot3(texts, images, NT)
    logits = value(0) * sums + value(1)
    row = lax.broadcasted_iota(jnp.int32, (WIN * ROWS, 1), 0)
    offset = jnp.where(
        row < ROWS,
        value(base),
        jnp.where(row < 2 * ROWS, value(base + 1) - ROWS, value(base + 2) - 2 * ROWS),
    )
    index = row.astype(jnp.float32) + offset
    positive = (index == labels).astype(jnp.float32)
    return split(jax.nn.sigmoid(logits) - positive)


def pack_kernel(images, labels, out, row, sem):
    images_in = pltpu.make_async_copy(images, out.at[pl.ds(0, ROWS), :], sem.at[0])
    label_in = pltpu.make_async_copy(labels, row, sem.at[1])
    images_in.start()
    label_in.start()
    label_in.wait()
    wide = row[...].astype(jnp.float32)
    wide = jnp.concatenate([wide, wide], axis=1)
    wide = jnp.concatenate([wide] * (D // (2 * ROWS)), axis=1)
    out[ROWS:, :] = jnp.broadcast_to(wide, (PACK - ROWS, D))
    images_in.wait()


def unit_kernel(text, unit):
    for r in range(0, ROWS, 32):
        unit[r : r + 32, :] = unit_rows(text[r : r + 32, :])


def early_kernel(
    log_scale, logit_bias, places, t0, u1, scalars, units, t_high, t_low, numbers, sem
):
    copies = [
        pltpu.make_async_copy(log_scale, numbers.at[0], sem.at[0]),
        pltpu.make_async_copy(logit_bias, numbers.at[1], sem.at[1]),
    ]
    for copy in copies:
        copy.start()
    for r in range(0, 2 * ROWS, 32):
        unit = unit_rows(t0[r : r + 32, :]) if r < ROWS else u1[r - ROWS : r - ROWS + 32, :]
        units[r : r + 32, :] = unit
        t_high[r : r + 32, :], t_low[r : r + 32, :] = split(unit)
    for copy in copies:
        copy.wait()

    def wide(value):
        return jnp.full((1, scalars.shape[1]), value, jnp.float32)

    scalars[0:1, :] = jnp.exp(wide(numbers[0, 0]))
    scalars[1:2, :] = wide(numbers[1, 0])
    for k in range(2 * WIN):
        scalars[2 + k : 3 + k, :] = wide(places[k].astype(jnp.float32))


def late_kernel(u2, early_units, early_high, early_low, units, t_high, t_low):
    early = 2 * ROWS
    units[:early, :] = early_units[...]
    t_high[:early, :] = early_high[...]
    t_low[:early, :] = early_low[...]
    units[early:, :] = u2[...]
    t_high[early:, :], t_low[early:, :] = split(u2[...])


def own_kernel(
    scalars, p0, p1, p2, p3, t_high, t_low, x_high, x_low, labels, w_high, w_low, grad_text
):
    packs = (p0, p1, p2, p3)
    for k, pack in enumerate(packs):
        for r in range(0, ROWS, 32):
            at = k * ROWS + r
            x_high[at : at + 32, :], x_low[at : at + 32, :] = split(
                unit_rows(pack[r : r + 32, :])
            )
    row = label_row(packs)
    labels[...] = jnp.broadcast_to(row, labels.shape)
    images = (x_high[...], x_low[...])
    weight = weights((t_high[...], t_low[...]), images, row, scalars, 2)
    w_high[...], w_low[...] = weight
    grad_text[...] = dot3(weight, images, NN)


def cross_kernel(
    scalars, units, x_high, x_low, labels, t_high, t_low, w_high, w_low, grad_text
):
    for at in range(0, WIN * ROWS, 32):
        t_high[at : at + 32, :], t_low[at : at + 32, :] = split(units[at : at + 32, :])
    images = (x_high[...], x_low[...])
    weight = weights((t_high[...], t_low[...]), images, labels[0:1, :], scalars, 5)
    w_high[...], w_low[...] = weight
    grad_text[...] = dot3(weight, images, NN)


def image_kernel(
    w_high, w_low, t_high, t_low, ow_high, ow_low, ot_high, ot_low, o0, o1, o2, o3
):
    total = dot3((w_high[...], w_low[...]), (t_high[...], t_low[...]), TN) + dot3(
        (ow_high[...], ow_low[...]), (ot_high[...], ot_low[...]), TN
    )
    for k, out in enumerate((o0, o1, o2, o3)):
        out[...] = total[k * ROWS : (k + 1) * ROWS, :]


def last_kernel(own, other, image_part, out, passed):
    at = (WIN - 1) * ROWS
    out[...] = own[at:, :] + other[at:, :]
    passed[...] = image_part[...]


def middle_kernel(back, moved, own, other, part, out_text, out_image):
    out_text[...] = (own[ROWS : 2 * ROWS, :] + other[ROWS : 2 * ROWS, :]) + back[...]
    out_image[...] = part[...] + moved[...]


def finish(values, grad, temper):
    inverse = lax.rsqrt(jnp.sum(values * values, axis=-1, keepdims=True) + EPS)
    unit = values * inverse
    grad = temper * grad
    along = jnp.sum(unit * grad, axis=-1, keepdims=True)
    return inverse * (grad - unit * along)


def final_kernel(
    scalars, images, captions, i0, i1, i3, own, other, back, out_images, out_captions
):
    temper = scalars[0:1, 0:1]
    for r in range(0, ROWS, 32):
        at = slice(r, r + 32)
        grad = (own[at, :] + other[at, :]) + back[at, :]
        out_captions[at, :] = finish(captions[at, :], grad, temper)
        grad = (i0[at, :] + i1[at, :]) + i3[at, :]
        out_images[at, :] = finish(images[at, :], grad, temper)


SMEM = pl.BlockSpec(memory_space=pltpu.SMEM)
VMEM = pl.BlockSpec(memory_space=pltpu.VMEM)
HBM = pl.BlockSpec(memory_space=pl.ANY)


def f32(*shape):
    return jax.ShapeDtypeStruct(shape, jnp.float32)


def b16(*shape):
    return jax.ShapeDtypeStruct(shape, jnp.bfloat16)


def call(kernel, inputs, outs, products, smem=0):
    return pl.pallas_call(
        kernel,
        in_specs=[SMEM] * smem + [VMEM] * (inputs - smem),
        out_specs=[VMEM] * len(outs),
        out_shape=outs,
        compiler_params=pltpu.CompilerParams(vmem_limit_bytes=VMEM_LIMIT),
        cost_estimate=pl.CostEstimate(
            flops=products * 3 * 2 * X * ROWS * WIN * ROWS * D,
            bytes_accessed=6 * X * ROWS * D * 4,
            transcendentals=X * ROWS * WIN * ROWS,
        ),
        name=kernel.__name__,
    )


def per_device(images, captions, labels, log_scale, logit_bias):
    position = lax.axis_index("loop")
    cycle_size = lax.axis_size("loop")
    member = lax.axis_index("group")
    members = lax.axis_size("group")
    images_all = X * ROWS
    texts_all = WIN * ROWS
    image_halves = [b16(images_all, D)] * 2
    text_halves = [b16(texts_all, D)] * 2

    text1 = along_loop(captions, 1)
    unit1 = pl.pallas_call(
        unit_kernel,
        in_specs=[VMEM],
        out_specs=VMEM,
        out_shape=f32(ROWS, D),
        compiler_params=pltpu.CompilerParams(vmem_limit_bytes=VMEM_LIMIT),
        cost_estimate=pl.CostEstimate(flops=2000000000, bytes_accessed=ROWS * D * 8, transcendentals=ROWS),
        name="unit_kernel",
    )(text1)
    unit2 = along_loop(unit1, 1)
    pack = pl.pallas_call(
        pack_kernel,
        in_specs=[HBM, HBM],
        out_specs=VMEM,
        out_shape=f32(PACK, D),
        scratch_shapes=[pltpu.VMEM((1, ROWS), jnp.int32), pltpu.SemaphoreType.DMA((2,))],
        compiler_params=pltpu.CompilerParams(vmem_limit_bytes=VMEM_LIMIT),
        name="pack_kernel",
    )(images, labels[None, :])
    pack1 = along_x(pack, 1)
    pack3 = along_x(pack, -1)
    pack2 = along_x(pack1, 1)

    places = []
    for who in (member, member ^ 1):
        for stride in range(WIN):
            source = (position - stride) % cycle_size
            places.append(source * (members * ROWS) + who * ROWS)
    places = jnp.stack(places)
    scalars, *early = pl.pallas_call(
        early_kernel,
        in_specs=[HBM, HBM, SMEM, VMEM, VMEM],
        out_specs=[VMEM] * 4,
        out_shape=[f32(8, 128), f32(2 * ROWS, D)] + [b16(2 * ROWS, D)] * 2,
        scratch_shapes=[pltpu.SMEM((2, 1), jnp.float32), pltpu.SemaphoreType.DMA((2,))],
        compiler_params=pltpu.CompilerParams(vmem_limit_bytes=VMEM_LIMIT),
        cost_estimate=pl.CostEstimate(
            flops=60 * 6 * X * ROWS * WIN * ROWS * D, bytes_accessed=6 * X * ROWS * D * 4, transcendentals=0
        ),
        name="early_kernel",
    )(log_scale, logit_bias, places, captions, unit1)
    units, t_high, t_low = call(late_kernel, 4, [f32(texts_all, D)] + text_halves, 0)(
        unit2, *early
    )
    other_units = across_cores(units)

    weight_halves = [b16(texts_all, images_all)] * 2
    x_high, x_low, label_rows, w_high, w_low, own_text = call(
        own_kernel,
        7,
        image_halves + [f32(8, images_all)] + weight_halves + [f32(texts_all, D)],
        60,
    )(scalars, pack, pack1, pack2, pack3, t_high, t_low)
    ot_high, ot_low, ow_high, ow_low, other_text = call(
        cross_kernel, 5, text_halves + weight_halves + [f32(texts_all, D)], 2
    )(scalars, other_units, x_high, x_low, label_rows)
    other_text = across_cores(other_text)
    i0, i1, i2, i3 = call(image_kernel, 8, [f32(ROWS, D)] * X, 2)(
        w_high, w_low, t_high, t_low, ow_high, ow_low, ot_high, ot_low
    )
    back, i2 = pl.pallas_call(
        last_kernel,
        in_specs=[VMEM] * 3,
        out_specs=[VMEM] * 2,
        out_shape=[f32(ROWS, D)] * 2,
        compiler_params=pltpu.CompilerParams(vmem_limit_bytes=VMEM_LIMIT),
        name="last_kernel",
    )(own_text, other_text, i2)
    back = along_loop(back, -1)
    moved = along_x(i2, -1)
    back, i1 = call(middle_kernel, 5, [f32(ROWS, D)] * 2, 0)(
        back, moved, own_text, other_text, i1
    )
    i1 = along_x(i1, -1)
    back = along_loop(back, -1)
    i3 = along_x(i3, 1)

    first = pl.BlockSpec((ROWS, D), lambda i: (0, 0))
    return tuple(
        pl.pallas_call(
            final_kernel,
            grid=(1,),
            in_specs=[pl.BlockSpec((8, 128), lambda i: (0, 0))] + [first] * 8,
            out_specs=[first] * 2,
            out_shape=[f32(ROWS, D)] * 2,
            compiler_params=pltpu.CompilerParams(vmem_limit_bytes=VMEM_LIMIT),
            name="finish",
        )(scalars, images, captions, i0, i1, i3, own_text, other_text, back)
    )


def solution(mesh):
    rows = P(("loop", "group"), None)
    placed = (rows, rows, P(("loop", "group")), P(), P())
    return jax.shard_map(
        per_device, mesh=mesh, in_specs=placed, out_specs=(rows, rows), check_vma=False
    )
```

```python
import jax
import jax.numpy as jnp
from jax import lax
from jax.experimental import pallas as pl
from jax.experimental.pallas import tpu as pltpu
from jax.sharding import PartitionSpec as P

WIN = 3
ROWS = 64
PACK = 72
D = 1152
X = 4
EPS = 1e-06
VMEM_LIMIT = 12 * 1024 * 1024


def along_loop(shard, by):
    count = lax.axis_size("loop")
    return lax.ppermute(shard, "loop", [(i, (i + by) % count) for i in range(count)])


def along_x(shard, by):
    count = lax.axis_size("group")
    pairs = [(i, (i + (2 * by if i % 2 == 0 else -2 * by)) % count) for i in range(count)]
    return lax.ppermute(shard, "group", pairs)


def across_cores(shard):
    count = lax.axis_size("group")
    return lax.ppermute(shard, "group", [(i, i ^ 1) for i in range(count)])


def split(values):
    high = values.astype(jnp.bfloat16)
    low = (values - high.astype(jnp.float32)).astype(jnp.bfloat16)
    return high, low


NT = (((1,), (1,)), ((), ()))
NN = (((1,), (0,)), ((), ()))
TN = (((0,), (0,)), ((), ()))


def dot3(a, b, dims):
    def one(left, right):
        return lax.dot_general(left, right, dims, preferred_element_type=jnp.float32)

    return one(a[0], b[0]) + (one(a[0], b[1]) + one(a[1], b[0]))


def unit_rows(values):
    return values * lax.rsqrt(jnp.sum(values * values, axis=-1, keepdims=True) + EPS)


def label_row(packs):
    width = X * ROWS
    lane = lax.broadcasted_iota(jnp.int32, (1, width), 1)
    rows = [pack[ROWS : ROWS + 1, :width] for pack in packs]
    result = rows[X - 1]
    for k in range(X - 2, -1, -1):
        result = jnp.where(lane < (k + 1) * ROWS, rows[k], result)
    return result


def weights(texts, images, labels, scalars, base):
    def value(at):
        return scalars[at : at + 1, 0:1]

    sums = dot3(texts, images, NT)
    logits = value(0) * sums + value(1)
    row = lax.broadcasted_iota(jnp.int32, (WIN * ROWS, 1), 0)
    offset = jnp.where(
        row < ROWS,
        value(base),
        jnp.where(row < 2 * ROWS, value(base + 1) - ROWS, value(base + 2) - 2 * ROWS),
    )
    index = row.astype(jnp.float32) + offset
    positive = (index == labels).astype(jnp.float32)
    return split(jax.nn.sigmoid(logits) - positive)


def pack_kernel(images, labels, out, row, sem):
    images_in = pltpu.make_async_copy(images, out.at[pl.ds(0, ROWS), :], sem.at[0])
    label_in = pltpu.make_async_copy(labels, row, sem.at[1])
    images_in.start()
    label_in.start()
    label_in.wait()
    wide = row[...].astype(jnp.float32)
    wide = jnp.concatenate([wide, wide], axis=1)
    wide = jnp.concatenate([wide] * (D // (2 * ROWS)), axis=1)
    out[ROWS:, :] = jnp.broadcast_to(wide, (PACK - ROWS, D))
    images_in.wait()


def unit_kernel(text, unit):
    for r in range(0, ROWS, 32):
        unit[r : r + 32, :] = unit_rows(text[r : r + 32, :])


def early_kernel(
    log_scale, logit_bias, places, t0, u1, scalars, units, t_high, t_low, numbers, sem
):
    copies = [
        pltpu.make_async_copy(log_scale, numbers.at[0], sem.at[0]),
        pltpu.make_async_copy(logit_bias, numbers.at[1], sem.at[1]),
    ]
    for copy in copies:
        copy.start()
    for r in range(0, 2 * ROWS, 32):
        unit = unit_rows(t0[r : r + 32, :]) if r < ROWS else u1[r - ROWS : r - ROWS + 32, :]
        units[r : r + 32, :] = unit
        t_high[r : r + 32, :], t_low[r : r + 32, :] = split(unit)
    for copy in copies:
        copy.wait()

    def wide(value):
        return jnp.full((1, scalars.shape[1]), value, jnp.float32)

    scalars[0:1, :] = jnp.exp(wide(numbers[0, 0]))
    scalars[1:2, :] = wide(numbers[1, 0])
    for k in range(2 * WIN):
        scalars[2 + k : 3 + k, :] = wide(places[k].astype(jnp.float32))


def late_kernel(u2, early_units, early_high, early_low, units, t_high, t_low):
    early = 2 * ROWS
    units[:early, :] = early_units[...]
    t_high[:early, :] = early_high[...]
    t_low[:early, :] = early_low[...]
    units[early:, :] = u2[...]
    t_high[early:, :], t_low[early:, :] = split(u2[...])


def own_kernel(
    scalars, p0, p1, p2, p3, t_high, t_low, x_high, x_low, labels, w_high, w_low, grad_text
):
    packs = (p0, p1, p2, p3)
    for k, pack in enumerate(packs):
        for r in range(0, ROWS, 32):
            at = k * ROWS + r
            x_high[at : at + 32, :], x_low[at : at + 32, :] = split(
                unit_rows(pack[r : r + 32, :])
            )
    row = label_row(packs)
    labels[...] = jnp.broadcast_to(row, labels.shape)
    images = (x_high[...], x_low[...])
    weight = weights((t_high[...], t_low[...]), images, row, scalars, 2)
    w_high[...], w_low[...] = weight
    grad_text[...] = dot3(weight, images, NN)


def cross_kernel(
    scalars, units, x_high, x_low, labels, t_high, t_low, w_high, w_low, grad_text
):
    for at in range(0, WIN * ROWS, 32):
        t_high[at : at + 32, :], t_low[at : at + 32, :] = split(units[at : at + 32, :])
    images = (x_high[...], x_low[...])
    weight = weights((t_high[...], t_low[...]), images, labels[0:1, :], scalars, 5)
    w_high[...], w_low[...] = weight
    grad_text[...] = dot3(weight, images, NN)


def image_kernel(
    w_high, w_low, t_high, t_low, ow_high, ow_low, ot_high, ot_low, o0, o1, o2, o3
):
    total = dot3((w_high[...], w_low[...]), (t_high[...], t_low[...]), TN) + dot3(
        (ow_high[...], ow_low[...]), (ot_high[...], ot_low[...]), TN
    )
    for k, out in enumerate((o0, o1, o2, o3)):
        out[...] = total[k * ROWS : (k + 1) * ROWS, :]


def last_kernel(own, other, after, out1, out2):
    out1[...] = own[ROWS : 2 * ROWS, :] + other[ROWS : 2 * ROWS, :]
    out2[...] = own[2 * ROWS :, :] + other[2 * ROWS :, :]


def sum_kernel(own, other, back1, back2, out):
    out[...] = (own[:ROWS, :] + other[:ROWS, :]) + (back1[...] + back2[...])


def finish(values, grad, temper):
    inverse = lax.rsqrt(jnp.sum(values * values, axis=-1, keepdims=True) + EPS)
    unit = values * inverse
    grad = temper * grad
    along = jnp.sum(unit * grad, axis=-1, keepdims=True)
    return inverse * (grad - unit * along)


def final_kernel(
    scalars, images, captions, grad_text, i0, i2, i1, i3, out_images, out_captions
):
    temper = scalars[0:1, 0:1]
    for r in range(0, ROWS, 32):
        at = slice(r, r + 32)
        out_captions[at, :] = finish(captions[at, :], grad_text[at, :], temper)
        grad = (i0[at, :] + i2[at, :]) + (i1[at, :] + i3[at, :])
        out_images[at, :] = finish(images[at, :], grad, temper)


SMEM = pl.BlockSpec(memory_space=pltpu.SMEM)
VMEM = pl.BlockSpec(memory_space=pltpu.VMEM)
HBM = pl.BlockSpec(memory_space=pl.ANY)


def f32(*shape):
    return jax.ShapeDtypeStruct(shape, jnp.float32)


def b16(*shape):
    return jax.ShapeDtypeStruct(shape, jnp.bfloat16)


def call(kernel, inputs, outs, products, smem=0):
    return pl.pallas_call(
        kernel,
        in_specs=[SMEM] * smem + [VMEM] * (inputs - smem),
        out_specs=[VMEM] * len(outs),
        out_shape=outs,
        compiler_params=pltpu.CompilerParams(vmem_limit_bytes=VMEM_LIMIT),
        cost_estimate=pl.CostEstimate(
            flops=products * 3 * 2 * X * ROWS * WIN * ROWS * D,
            bytes_accessed=6 * X * ROWS * D * 4,
            transcendentals=X * ROWS * WIN * ROWS,
        ),
        name=kernel.__name__,
    )


def per_device(images, captions, labels, log_scale, logit_bias):
    position = lax.axis_index("loop")
    cycle_size = lax.axis_size("loop")
    member = lax.axis_index("group")
    members = lax.axis_size("group")
    images_all = X * ROWS
    texts_all = WIN * ROWS
    image_halves = [b16(images_all, D)] * 2
    text_halves = [b16(texts_all, D)] * 2

    text1 = along_loop(captions, 1)
    unit1 = pl.pallas_call(
        unit_kernel,
        in_specs=[VMEM],
        out_specs=VMEM,
        out_shape=f32(ROWS, D),
        compiler_params=pltpu.CompilerParams(vmem_limit_bytes=VMEM_LIMIT),
        cost_estimate=pl.CostEstimate(flops=2000000000, bytes_accessed=ROWS * D * 8, transcendentals=ROWS),
        name="unit_kernel",
    )(text1)
    unit2 = along_loop(unit1, 1)
    pack = pl.pallas_call(
        pack_kernel,
        in_specs=[HBM, HBM],
        out_specs=VMEM,
        out_shape=f32(PACK, D),
        scratch_shapes=[pltpu.VMEM((1, ROWS), jnp.int32), pltpu.SemaphoreType.DMA((2,))],
        compiler_params=pltpu.CompilerParams(vmem_limit_bytes=VMEM_LIMIT),
        name="pack_kernel",
    )(images, labels[None, :])
    pack1 = along_x(pack, 1)
    pack3 = along_x(pack, -1)
    pack2 = along_x(pack1, 1)

    places = []
    for who in (member, member ^ 1):
        for stride in range(WIN):
            source = (position - stride) % cycle_size
            places.append(source * (members * ROWS) + who * ROWS)
    places = jnp.stack(places)
    scalars, *early = pl.pallas_call(
        early_kernel,
        in_specs=[HBM, HBM, SMEM, VMEM, VMEM],
        out_specs=[VMEM] * 4,
        out_shape=[f32(8, 128), f32(2 * ROWS, D)] + [b16(2 * ROWS, D)] * 2,
        scratch_shapes=[pltpu.SMEM((2, 1), jnp.float32), pltpu.SemaphoreType.DMA((2,))],
        compiler_params=pltpu.CompilerParams(vmem_limit_bytes=VMEM_LIMIT),
        cost_estimate=pl.CostEstimate(
            flops=60 * 6 * X * ROWS * WIN * ROWS * D, bytes_accessed=6 * X * ROWS * D * 4, transcendentals=0
        ),
        name="early_kernel",
    )(log_scale, logit_bias, places, captions, unit1)
    units, t_high, t_low = call(late_kernel, 4, [f32(texts_all, D)] + text_halves, 0)(
        unit2, *early
    )
    other_units = across_cores(units)

    weight_halves = [b16(texts_all, images_all)] * 2
    x_high, x_low, label_rows, w_high, w_low, own_text = call(
        own_kernel,
        7,
        image_halves + [f32(8, images_all)] + weight_halves + [f32(texts_all, D)],
        60,
    )(scalars, pack, pack1, pack2, pack3, t_high, t_low)
    ot_high, ot_low, ow_high, ow_low, other_text = call(
        cross_kernel, 5, text_halves + weight_halves + [f32(texts_all, D)], 2
    )(scalars, other_units, x_high, x_low, label_rows)
    other_text = across_cores(other_text)
    i0, i1, i2, i3 = call(image_kernel, 8, [f32(ROWS, D)] * X, 2)(
        w_high, w_low, t_high, t_low, ow_high, ow_low, ot_high, ot_low
    )
    back1, back2 = pl.pallas_call(
        last_kernel,
        in_specs=[VMEM, VMEM, HBM],
        out_specs=[VMEM] * 2,
        out_shape=[f32(ROWS, D)] * 2,
        compiler_params=pltpu.CompilerParams(vmem_limit_bytes=VMEM_LIMIT),
        name="last_kernel",
    )(own_text, other_text, i0)
    back2 = along_loop(back2, -2)
    back1 = along_loop(back1, -1)
    (grad_text,) = call(sum_kernel, 4, [f32(ROWS, D)], 1)(own_text, other_text, back1, back2)
    i2 = along_x(i2, 2)
    i1 = along_x(i1, -1)
    i3 = along_x(i3, 1)

    first = pl.BlockSpec((ROWS, D), lambda i: (0, 0))
    return tuple(
        pl.pallas_call(
            final_kernel,
            grid=(1,),
            in_specs=[pl.BlockSpec((8, 128), lambda i: (0, 0))] + [first] * 7,
            out_specs=[first] * 2,
            out_shape=[f32(ROWS, D)] * 2,
            compiler_params=pltpu.CompilerParams(vmem_limit_bytes=VMEM_LIMIT),
            name="finish",
        )(scalars, images, captions, grad_text, i0, i2, i1, i3)
    )


def solution(mesh):
    rows = P(("loop", "group"), None)
    placed = (rows, rows, P(("loop", "group")), P(), P())
    return jax.shard_map(
        per_device, mesh=mesh, in_specs=placed, out_specs=(rows, rows), check_vma=False
    )
```

```python
import jax
import jax.numpy as jnp
from jax import lax
from jax.experimental import pallas as pl
from jax.experimental.pallas import tpu as pltpu
from jax.sharding import PartitionSpec as P

WIN = 3
ROWS = 64
PACK = 72
D = 1152
X = 4
EPS = 1e-06
VMEM_LIMIT = 12 * 1024 * 1024


def along_loop(shard, by):
    count = lax.axis_size("loop")
    return lax.ppermute(shard, "loop", [(i, (i + by) % count) for i in range(count)])


def along_x(shard, by):
    count = lax.axis_size("group")
    pairs = [(i, (i + (2 * by if i % 2 == 0 else -2 * by)) % count) for i in range(count)]
    return lax.ppermute(shard, "group", pairs)


def across_cores(shard):
    count = lax.axis_size("group")
    return lax.ppermute(shard, "group", [(i, i ^ 1) for i in range(count)])


def split(values):
    high = values.astype(jnp.bfloat16)
    low = (values - high.astype(jnp.float32)).astype(jnp.bfloat16)
    return high, low


NT = (((1,), (1,)), ((), ()))
NN = (((1,), (0,)), ((), ()))
TN = (((0,), (0,)), ((), ()))


def dot3(a, b, dims):
    def one(left, right):
        return lax.dot_general(left, right, dims, preferred_element_type=jnp.float32)

    return one(a[0], b[0]) + (one(a[0], b[1]) + one(a[1], b[0]))


def unit_rows(values):
    return values * lax.rsqrt(jnp.sum(values * values, axis=-1, keepdims=True) + EPS)


def label_row(packs):
    width = X * ROWS
    lane = lax.broadcasted_iota(jnp.int32, (1, width), 1)
    rows = [pack[ROWS : ROWS + 1, :width] for pack in packs]
    result = rows[X - 1]
    for k in range(X - 2, -1, -1):
        result = jnp.where(lane < (k + 1) * ROWS, rows[k], result)
    return result


def weights(texts, images, labels, scalars, base):
    def value(at):
        return scalars[at : at + 1, 0:1]

    sums = dot3(texts, images, NT)
    logits = value(0) * sums + value(1)
    row = lax.broadcasted_iota(jnp.int32, (WIN * ROWS, 1), 0)
    offset = jnp.where(
        row < ROWS,
        value(base),
        jnp.where(row < 2 * ROWS, value(base + 1) - ROWS, value(base + 2) - 2 * ROWS),
    )
    index = row.astype(jnp.float32) + offset
    positive = (index == labels).astype(jnp.float32)
    return split(jax.nn.sigmoid(logits) - positive)


def pack_kernel(images, labels, out, row, sem):
    images_in = pltpu.make_async_copy(images, out.at[pl.ds(0, ROWS), :], sem.at[0])
    label_in = pltpu.make_async_copy(labels, row, sem.at[1])
    images_in.start()
    label_in.start()
    label_in.wait()
    wide = row[...].astype(jnp.float32)
    wide = jnp.concatenate([wide, wide], axis=1)
    wide = jnp.concatenate([wide] * (D // (2 * ROWS)), axis=1)
    out[ROWS:, :] = jnp.broadcast_to(wide, (PACK - ROWS, D))
    images_in.wait()


def unit_kernel(text, unit):
    for r in range(0, ROWS, 32):
        unit[r : r + 32, :] = unit_rows(text[r : r + 32, :])


def early_kernel(
    log_scale, logit_bias, places, t0, u1, scalars, units, t_high, t_low, numbers, sem
):
    copies = [
        pltpu.make_async_copy(log_scale, numbers.at[0], sem.at[0]),
        pltpu.make_async_copy(logit_bias, numbers.at[1], sem.at[1]),
    ]
    for copy in copies:
        copy.start()
    for r in range(0, 2 * ROWS, 32):
        unit = unit_rows(t0[r : r + 32, :]) if r < ROWS else u1[r - ROWS : r - ROWS + 32, :]
        units[r : r + 32, :] = unit
        t_high[r : r + 32, :], t_low[r : r + 32, :] = split(unit)
    for copy in copies:
        copy.wait()

    def wide(value):
        return jnp.full((1, scalars.shape[1]), value, jnp.float32)

    scalars[0:1, :] = jnp.exp(wide(numbers[0, 0]))
    scalars[1:2, :] = wide(numbers[1, 0])
    for k in range(2 * WIN):
        scalars[2 + k : 3 + k, :] = wide(places[k].astype(jnp.float32))


def late_kernel(u2, early_units, early_high, early_low, units, t_high, t_low):
    early = 2 * ROWS
    units[:early, :] = early_units[...]
    t_high[:early, :] = early_high[...]
    t_low[:early, :] = early_low[...]
    units[early:, :] = u2[...]
    t_high[early:, :], t_low[early:, :] = split(u2[...])


def own_kernel(
    scalars, p0, p1, p2, p3, t_high, t_low, x_high, x_low, labels, w_high, w_low, grad_text
):
    packs = (p0, p1, p2, p3)
    for k, pack in enumerate(packs):
        for r in range(0, ROWS, 32):
            at = k * ROWS + r
            x_high[at : at + 32, :], x_low[at : at + 32, :] = split(
                unit_rows(pack[r : r + 32, :])
            )
    row = label_row(packs)
    labels[...] = jnp.broadcast_to(row, labels.shape)
    images = (x_high[...], x_low[...])
    weight = weights((t_high[...], t_low[...]), images, row, scalars, 2)
    w_high[...], w_low[...] = weight
    grad_text[...] = dot3(weight, images, NN)


def cross_kernel(
    scalars, units, x_high, x_low, labels, t_high, t_low, w_high, w_low, grad_text
):
    for at in range(0, WIN * ROWS, 32):
        t_high[at : at + 32, :], t_low[at : at + 32, :] = split(units[at : at + 32, :])
    images = (x_high[...], x_low[...])
    weight = weights((t_high[...], t_low[...]), images, labels[0:1, :], scalars, 5)
    w_high[...], w_low[...] = weight
    grad_text[...] = dot3(weight, images, NN)


def image_kernel(
    w_high, w_low, t_high, t_low, ow_high, ow_low, ot_high, ot_low, o0, o1, o2, o3
):
    total = dot3((w_high[...], w_low[...]), (t_high[...], t_low[...]), TN) + dot3(
        (ow_high[...], ow_low[...]), (ot_high[...], ot_low[...]), TN
    )
    for k, out in enumerate((o0, o1, o2, o3)):
        out[...] = total[k * ROWS : (k + 1) * ROWS, :]


def last_kernel(own, other, after, out1, out2):
    out1[...] = own[ROWS : 2 * ROWS, :] + other[ROWS : 2 * ROWS, :]
    out2[...] = own[2 * ROWS :, :] + other[2 * ROWS :, :]


def add_kernel(a, b, out):
    out[...] = a[...] + b[...]


def sum_kernel(own, other, back1, back2, out):
    out[...] = (own[:ROWS, :] + other[:ROWS, :]) + (back1[...] + back2[...])


def finish(values, grad, temper):
    inverse = lax.rsqrt(jnp.sum(values * values, axis=-1, keepdims=True) + EPS)
    unit = values * inverse
    grad = temper * grad
    along = jnp.sum(unit * grad, axis=-1, keepdims=True)
    return inverse * (grad - unit * along)


def final_kernel(
    scalars, images, captions, i0, i1, i3, grad_text, out_images, out_captions
):
    temper = scalars[0:1, 0:1]
    for r in range(0, ROWS, 32):
        at = slice(r, r + 32)
        out_captions[at, :] = finish(captions[at, :], grad_text[at, :], temper)
        grad = (i0[at, :] + i1[at, :]) + i3[at, :]
        out_images[at, :] = finish(images[at, :], grad, temper)


SMEM = pl.BlockSpec(memory_space=pltpu.SMEM)
VMEM = pl.BlockSpec(memory_space=pltpu.VMEM)
HBM = pl.BlockSpec(memory_space=pl.ANY)


def f32(*shape):
    return jax.ShapeDtypeStruct(shape, jnp.float32)


def b16(*shape):
    return jax.ShapeDtypeStruct(shape, jnp.bfloat16)


def call(kernel, inputs, outs, products, smem=0):
    return pl.pallas_call(
        kernel,
        in_specs=[SMEM] * smem + [VMEM] * (inputs - smem),
        out_specs=[VMEM] * len(outs),
        out_shape=outs,
        compiler_params=pltpu.CompilerParams(vmem_limit_bytes=VMEM_LIMIT),
        cost_estimate=pl.CostEstimate(
            flops=products * 3 * 2 * X * ROWS * WIN * ROWS * D,
            bytes_accessed=6 * X * ROWS * D * 4,
            transcendentals=X * ROWS * WIN * ROWS,
        ),
        name=kernel.__name__,
    )


def per_device(images, captions, labels, log_scale, logit_bias):
    position = lax.axis_index("loop")
    cycle_size = lax.axis_size("loop")
    member = lax.axis_index("group")
    members = lax.axis_size("group")
    images_all = X * ROWS
    texts_all = WIN * ROWS
    image_halves = [b16(images_all, D)] * 2
    text_halves = [b16(texts_all, D)] * 2

    text1 = along_loop(captions, 1)
    unit1 = pl.pallas_call(
        unit_kernel,
        in_specs=[VMEM],
        out_specs=VMEM,
        out_shape=f32(ROWS, D),
        compiler_params=pltpu.CompilerParams(vmem_limit_bytes=VMEM_LIMIT),
        cost_estimate=pl.CostEstimate(flops=2000000000, bytes_accessed=ROWS * D * 8, transcendentals=ROWS),
        name="unit_kernel",
    )(text1)
    unit2 = along_loop(unit1, 1)
    pack = pl.pallas_call(
        pack_kernel,
        in_specs=[HBM, HBM],
        out_specs=VMEM,
        out_shape=f32(PACK, D),
        scratch_shapes=[pltpu.VMEM((1, ROWS), jnp.int32), pltpu.SemaphoreType.DMA((2,))],
        compiler_params=pltpu.CompilerParams(vmem_limit_bytes=VMEM_LIMIT),
        name="pack_kernel",
    )(images, labels[None, :])
    pack1 = along_x(pack, 1)
    pack3 = along_x(pack, -1)
    pack2 = along_x(pack1, 1)

    places = []
    for who in (member, member ^ 1):
        for stride in range(WIN):
            source = (position - stride) % cycle_size
            places.append(source * (members * ROWS) + who * ROWS)
    places = jnp.stack(places)
    scalars, *early = pl.pallas_call(
        early_kernel,
        in_specs=[HBM, HBM, SMEM, VMEM, VMEM],
        out_specs=[VMEM] * 4,
        out_shape=[f32(8, 128), f32(2 * ROWS, D)] + [b16(2 * ROWS, D)] * 2,
        scratch_shapes=[pltpu.SMEM((2, 1), jnp.float32), pltpu.SemaphoreType.DMA((2,))],
        compiler_params=pltpu.CompilerParams(vmem_limit_bytes=VMEM_LIMIT),
        cost_estimate=pl.CostEstimate(
            flops=60 * 6 * X * ROWS * WIN * ROWS * D, bytes_accessed=6 * X * ROWS * D * 4, transcendentals=0
        ),
        name="early_kernel",
    )(log_scale, logit_bias, places, captions, unit1)
    units, t_high, t_low = call(late_kernel, 4, [f32(texts_all, D)] + text_halves, 0)(
        unit2, *early
    )
    other_units = across_cores(units)

    weight_halves = [b16(texts_all, images_all)] * 2
    x_high, x_low, label_rows, w_high, w_low, own_text = call(
        own_kernel,
        7,
        image_halves + [f32(8, images_all)] + weight_halves + [f32(texts_all, D)],
        60,
    )(scalars, pack, pack1, pack2, pack3, t_high, t_low)
    ot_high, ot_low, ow_high, ow_low, other_text = call(
        cross_kernel, 5, text_halves + weight_halves + [f32(texts_all, D)], 2
    )(scalars, other_units, x_high, x_low, label_rows)
    other_text = across_cores(other_text)
    i0, i1, i2, i3 = call(image_kernel, 8, [f32(ROWS, D)] * X, 2)(
        w_high, w_low, t_high, t_low, ow_high, ow_low, ot_high, ot_low
    )
    back1, back2 = pl.pallas_call(
        last_kernel,
        in_specs=[VMEM, VMEM, HBM],
        out_specs=[VMEM] * 2,
        out_shape=[f32(ROWS, D)] * 2,
        compiler_params=pltpu.CompilerParams(vmem_limit_bytes=VMEM_LIMIT),
        name="last_kernel",
    )(own_text, other_text, i0)
    back2 = along_loop(back2, -2)
    back1 = along_loop(back1, -1)
    (grad_text,) = call(sum_kernel, 4, [f32(ROWS, D)], 60)(own_text, other_text, back1, back2)
    (i1,) = call(add_kernel, 2, [f32(ROWS, D)], 0)(i1, along_x(i2, -1))
    i1 = along_x(i1, -1)
    i3 = along_x(i3, 1)

    first = pl.BlockSpec((ROWS, D), lambda i: (0, 0))
    return tuple(
        pl.pallas_call(
            final_kernel,
            grid=(1,),
            in_specs=[pl.BlockSpec((8, 128), lambda i: (0, 0))] + [first] * 6,
            out_specs=[first] * 2,
            out_shape=[f32(ROWS, D)] * 2,
            compiler_params=pltpu.CompilerParams(vmem_limit_bytes=VMEM_LIMIT),
            name="finish",
        )(scalars, images, captions, i0, i1, i3, grad_text)
    )


def solution(mesh):
    rows = P(("loop", "group"), None)
    placed = (rows, rows, P(("loop", "group")), P(), P())
    return jax.shard_map(
        per_device, mesh=mesh, in_specs=placed, out_specs=(rows, rows), check_vma=False
    )
```
